256 devices in a mesh: row: 16 (over z_hi, x, core), col: 16 (over z_lo, y).
Axes of the slice: x: 4, y: 4, z: 8 (z_hi: 2, z_lo: 4; z = z_hi * 4 + z_lo), core: 2. Of those that a mesh axis runs over, the one named last changes fastest.
Arguments:
- basis: bfloat16 [65536, 2048], P('row', 'col'), may hold values from -0.375 to 0.375
- stiffness: bfloat16 [2, 1024, 64, 512], P(None, 'row'), may hold values from -0.25 to 0.25
- block_cols: int32 [1024, 8], P('row'), may hold values from 0 to 1023, as said below
- block_counts: int32 [1024], P('row'), may hold values from 3 to 8
Outputs:
- reduced: float32 [2048, 2, 2048], P('row', None, 'col')
The draws below stay inside these ranges and needn't reach their ends.
Inputs may be any that keep to these rules, and one draw needn't show every extreme that they name: `block_cols`: each entry lies within 2 of its block row's own index; slot 0 is the block row itself, slot 1 and slot 2 lie 2 before and after it (clipped to the mesh).
All inputs are finite; a program needn't handle non-finite values.
Results may differ from the reference program's by a relative error of at most 0.0029.
Values may be sent and summed in bfloat16 or wider, within the bound.
A program may use at most 128 MiB of HBM per device.

```python
import jax
import jax.numpy as jnp
from jax import lax

R = 2048
BLOCK = 64
CAP = 8
HB = 2
NDOF = 65536
NBT = 1024
N_COL = 16


def draw_block_cols(key, part):
    offsets = jax.random.randint(key, (NBT, CAP), -HB, HB + 1)
    slot = jnp.arange(CAP)[None, :]
    offsets = jnp.where(slot == 0, 0, jnp.where(slot == 1, -HB, jnp.where(slot == 2, HB, offsets)))
    base = jnp.arange(NBT)[:, None]
    return jnp.clip(base + offsets, 0, NBT - 1).astype(jnp.int32)


def draw_block_counts(key, part):
    counts = jax.random.randint(key, (NBT,), 3, CAP + 1)
    return jnp.where(jnp.arange(NBT) % 8 == 0, CAP, counts).astype(jnp.int32)


def block_scale(rng, shape, cuts, low, largest):
    def one(dim, shards_of):
        heights = jax.random.uniform(jax.random.fold_in(jax.random.fold_in(rng, 6), dim), (shards_of,), jnp.float32, low / len(cuts), largest / len(cuts))
        return jnp.repeat(jnp.exp(heights), shape[dim] // shards_of).reshape((-1,) + (1,) * (len(shape) - dim - 1))

    loudness = one(*cuts[0])
    for cut in cuts[1:]:
        loudness = loudness * one(*cut)
    return loudness


def scatter_about(rng, dims, scale, reach, split=(), held_as=jnp.bfloat16):
    values = jax.random.normal(rng, dims, jnp.float32) * scale
    if len(split) > 0:
        values = block_scale(rng, dims, split, -0.22, 0.18) * values
    return jnp.clip(values, min=-reach, max=reach).astype(held_as)


def setup_inputs(seed: int = 0) -> dict:
    key_of = jax.random.split(jax.random.key(seed), 5)
    basis = scatter_about(key_of[0], (NDOF, R), 256 ** -0.5, 0.375, ((0, 16), (1, 16)))
    stiffness = scatter_about(key_of[1], (2, NBT, BLOCK, CAP * BLOCK), (CAP * BLOCK) ** -0.5, 0.25, ((1, 16),))
    block_cols = draw_block_cols(jax.random.fold_in(key_of[4], 71), 0)
    block_counts = draw_block_counts(jax.random.fold_in(key_of[4], 71), 0)
    return {"basis": basis, "stiffness": stiffness, "block_cols": block_cols, "block_counts": block_counts}


def reference(basis, stiffness, block_cols, block_counts):
    ndof, width = basis.shape
    nblocks = ndof // BLOCK
    framed = basis.reshape(nblocks, BLOCK, width)
    slots = jnp.arange(CAP, dtype=jnp.int32)

    def one_row(inputs):
        blocks, cols, count = inputs
        live = (slots < count).astype(jnp.float32)
        picked = framed[cols.astype(jnp.int32)].astype(jnp.float32) * live[:, None, None]
        picked = picked.reshape(CAP * BLOCK, width)
        result = jnp.einsum("qrk,kp->qrp", blocks.astype(jnp.float32), picked, precision=lax.Precision.HIGHEST)
        return result.astype(jnp.bfloat16)

    applied = lax.map(one_row, (jnp.moveaxis(stiffness, 1, 0), block_cols, block_counts))
    applied = jnp.moveaxis(applied, 1, 0).reshape(2, ndof, width)
    panel = width // N_COL
    result = jnp.zeros((width, 2, width), jnp.float32)
    for column in range(N_COL):
        upper = (column + 1) * panel
        lower = column * panel
        right = jnp.concatenate([applied[0, :, lower:upper], applied[1, :, lower:upper]], axis=1)
        part = lax.dot_general(basis[:, :upper], right, (((0,), (0,)), ((), ())), preferred_element_type=jnp.float32)
        result = result.at[:upper, :, lower:upper].set(part.reshape(upper, 2, panel))
    return result
```

```python
import jax
import jax.numpy as jnp
from jax import lax
from jax.experimental import pallas as pl
from jax.experimental.pallas import tpu as pltpu
from jax.sharding import PartitionSpec as P

MESH = pl.DeviceIdType.MESH
BF = jnp.bfloat16
F32 = jnp.float32
BLOCK = 64
CAP = 8
HALO = 2 * BLOCK
ROWS = 4096
HALF = ROWS // 2
NB = HALF // BLOCK
EXT = HALF + 2 * HALO
DEAD = EXT // BLOCK
PAN = 128


def kernel(idx, basis_ref, stiff_ref, out_ref,
           sv, ox, ya, yh, zu, zd, g, pt, zt, ap, az, acc, r1, s2, r2, fin,
           lsem, hs, hr, fs, fr, ys, yr, zus, zur, zds, zdr, s1s, s1r, s2s, s2r, s3s, s3r):
    r = lax.axis_index("row")
    c = lax.axis_index("col")
    core, x, zh = r % 2, (r // 2) % 4, r // 8
    a, b = c // 4, c % 4

    load_own = pltpu.make_async_copy(basis_ref, ox.at[pl.ds(HALO, ROWS)], lsem.at[0])
    load_own.start()
    load_s = pltpu.make_async_copy(stiff_ref, sv, lsem.at[1])
    load_s.start()

    def yb(d):
        return (b + d) % 4

    def ycol(d):
        return a * 4 + yb(d)

    def zcol(z):
        return z * 4 + b

    up_row, down_row = (r + 1) % 16, (r + 15) % 16
    barrier = pltpu.get_barrier_semaphore()
    other_zh = (1 - zh) * 8 + x * 2 + core
    partners = [(up_row, c), (down_row, c), (other_zh, c)]
    partners += [(zh * 8 + ((x + d) % 4) * 2 + core, c) for d in (1, 2, 3)]
    for d in (1, 2, 3):
        for row in (r, other_zh):
            partners += [(row, ycol(d)), (row, zcol((a + d) % 4))]
    for dev in partners:
        pl.semaphore_signal(barrier, inc=1, device_id=dev, device_id_type=MESH)
    pl.semaphore_wait(barrier, len(partners))

    def remote(src, dst, ss, rs, dev):
        return pltpu.make_async_remote_copy(src_ref=src, dst_ref=dst, send_sem=ss, recv_sem=rs,
                                            device_id=dev, device_id_type=MESH)

    halo_up = remote(ox.at[pl.ds(ROWS, HALO)], ox.at[pl.ds(0, HALO)], hs.at[0], hr.at[0], (up_row, c))
    halo_down = remote(ox.at[pl.ds(HALO, HALO)], ox.at[pl.ds(ROWS + HALO, HALO)], hs.at[1], hr.at[1], (down_row, c))
    own_lo = ox.at[pl.ds(HALO, HALF)]
    own_hi = ox.at[pl.ds(HALO + HALF, HALF)]
    nxt, prv = (r, ycol(1)), (r, ycol(3))
    y_lo_n = remote(own_lo, ya.at[1, pl.ds(HALO, HALF)], ys.at[0], yr.at[0], nxt)
    y_hi_n = remote(own_hi, yh.at[1], ys.at[1], yr.at[1], nxt)
    y_hi_p = remote(own_hi, yh.at[0], ys.at[2], yr.at[2], prv)
    y_lo_p = remote(own_lo, ya.at[0, pl.ds(HALO, HALF)], ys.at[3], yr.at[3], prv)
    y_lo_f = remote(ya.at[1, pl.ds(HALO, HALF)], ya.at[2, pl.ds(HALO, HALF)], ys.at[4], yr.at[4], nxt)
    y_hi_f = remote(yh.at[0], yh.at[2], ys.at[5], yr.at[5], prv)

    zup = (r, zcol((a + 1) % 4))
    zdn = (r, zcol((a + 3) % 4))
    DN = HALF + HALO
    zu_cp = [remote(own_lo, zu.at[0], zus.at[0], zur.at[0], zup)]
    zd_cp = [remote(ox.at[pl.ds(HALF, DN)], zd.at[0, pl.ds(0, DN)], zds.at[0], zdr.at[0], zdn)]
    for d in (1, 2):
        zu_cp.append(remote(zu.at[d - 1], zu.at[d], zus.at[d], zur.at[d], zup))
        zd_cp.append(remote(zd.at[d - 1, pl.ds(0, DN)], zd.at[d, pl.ds(0, DN)], zds.at[d], zdr.at[d], zdn))

    load_own.wait()
    halo_up.start()
    halo_down.start()

    @pl.when(a < 3)
    def _():
        zu_cp[0].start()

    @pl.when(a > 0)
    def _():
        zd_cp[0].start()

    y_lo_n.start()
    y_hi_p.start()
    y_hi_n.start()
    y_lo_p.start()

    g[DEAD] = jnp.zeros((BLOCK, 2 * PAN), BF)

    halo_up.wait_recv()
    halo_down.wait_recv()
    fan_lo = [remote(ox.at[pl.ds(0, HALO)], ya.at[s - 1, pl.ds(0, HALO)], fs.at[s - 1], fr.at[s - 1], (r, ycol(dy)))
              for s, dy in ((1, 3), (2, 1), (3, 2))]
    fan_hi = [remote(ox.at[pl.ds(HALO + ROWS, HALO)], zd.at[d - 1, pl.ds(DN, HALO)], fs.at[2 + d], fr.at[2 + d],
                     (r, zcol((a + 4 - d) % 4))) for d in (1, 2, 3)]
    for cp in fan_lo:
        cp.start()
    for d in (1, 2, 3):
        @pl.when(a >= d)
        def _():
            fan_hi[d - 1].start()

    def apply(h, outs):
        n = len(outs) * PAN

        def step(i, carry):
            row = h * NB + i
            lhs = jnp.concatenate([sv[0, row], sv[1, row]], axis=0)
            picked = jnp.concatenate(
                [g[idx[row * CAP + s]][:, 0:n] for s in range(CAP)], axis=0)
            res = jnp.dot(lhs, picked, preferred_element_type=F32).astype(BF)
            at = pl.ds(pl.multiple_of(i * BLOCK, BLOCK), BLOCK)
            for p, (ref, k) in enumerate(outs):
                for q in range(2):
                    ref[k, at, q * PAN:(q + 1) * PAN] = res[q * BLOCK:(q + 1) * BLOCK, p * PAN:(p + 1) * PAN]
            return carry

        lax.fori_loop(0, NB, step, 0, unroll=2)

    def put(rows, at, lane):
        n = rows.shape[0] // BLOCK
        g[at:at + n, :, lane:lane + PAN] = rows.reshape(n, BLOCK, PAN)

    def take_y(s, lane):
        put(ya[s - 1], 0, lane)
        put(yh[s - 1, 0:HALO], DEAD - 2, lane)

    def turn_y(s):
        pt[0, s * PAN:(s + 1) * PAN, :] = ya[s - 1, HALO:HALO + HALF, :].T
        pt[1, s * PAN:(s + 1) * PAN, :] = yh[s - 1].T

    def down(d, lo, hi):
        res = jnp.dot(pt[1, lo * PAN:hi * PAN, :], az[d], preferred_element_type=F32)
        if d == 0:
            res += jnp.dot(pt[0, lo * PAN:hi * PAN, :], ap[0], preferred_element_type=F32)
        acc[a + d, lo * PAN:hi * PAN, :] = res

    def up(d, s):
        acc[a - d, s * PAN:(s + 1) * PAN, :] = jnp.dot(zt[d - 1], ap[s], preferred_element_type=F32)

    load_s.wait()
    put(ox[0:EXT, :], 0, 0)
    apply(0, [(ap, 0)])
    pt[0, 0:PAN, :] = ox[HALO:HALO + HALF, :].T
    pt[1, 0:PAN, :] = ox[HALO + HALF:HALO + ROWS, :].T

    @pl.when(a > 0)
    def _():
        zu_cp[0].wait_recv()

    @pl.when((a > 0) & (a < 3))
    def _():
        zu_cp[1].start()

    @pl.when(a < 3)
    def _():
        zd_cp[0].wait_recv()

    @pl.when((a < 3) & (a > 0))
    def _():
        zd_cp[1].start()

    y_lo_n.wait_recv()
    y_lo_f.start()
    y_hi_p.wait_recv()
    y_hi_f.start()

    put(ox[HALF:HALF + EXT, :], 0, 0)

    @pl.when(a < 3)
    def _():
        fan_hi[0].wait_recv()
        put(zd[0], 0, PAN)
        apply(1, [(az, 0), (az, 1)])

    @pl.when(a == 3)
    def _():
        apply(1, [(az, 0)])

    @pl.when(a > 1)
    def _():
        zu_cp[1].wait_recv()

    @pl.when(a == 2)
    def _():
        zu_cp[2].start()

    @pl.when(a < 2)
    def _():
        zd_cp[1].wait_recv()

    @pl.when(a == 1)
    def _():
        zd_cp[2].start()

    y_hi_n.wait_recv()
    y_lo_p.wait_recv()
    for s in (1, 2):
        fan_lo[s - 1].wait_recv()
        turn_y(s)

    @pl.when(a > 0)
    def _():
        take_y(1, 0)
        take_y(2, PAN)
        apply(0, [(ap, 1), (ap, 2)])
        zt[0] = zu[0].T
        for s in (0, 1, 2):
            up(1, s)

    @pl.when(a > 1)
    def _():
        zt[1] = zu[1].T
        for s in (0, 1, 2):
            up(2, s)

    down(0, 0, 3)

    @pl.when(a < 3)
    def _():
        down(1, 0, 3)

    @pl.when(a < 2)
    def _():
        fan_hi[1].wait_recv()
        put(zd[1], 0, 0)
        apply(1, [(az, 2)])
        down(2, 0, 3)

    def block(k):
        z, s = k // 4, k % 4
        y = (b + s + (s // 2) * (1 - 2 * (s % 2))) % 4
        left = jnp.where(z < a, z * 4 + b, a * 4 + y)
        right = jnp.where(z < a, a * 4 + y, z * 4 + b)
        used = (z != a) | (y <= b)
        early = (s != 3) & (z - a != 3) & (a - z != 3)
        return z, s, left, right, used, early

    def at(k):
        return acc.at[k // 4, pl.ds(pl.multiple_of((k % 4) * PAN, PAN), PAN), :]

    def pair_copy(k):
        return remote(at(k), r1.at[k], s1s.at[k], s1r.at[k], (zh * 8 + x * 2 + (1 - core), c))

    def x_copy(k, xp):
        place = (x - xp + 4) % 4 - 1
        return remote(s2.at[k], r2.at[k, place], s2s.at[k], s2r.at[k, place], (zh * 8 + xp * 2 + core, c))

    def last_copy(k, z, left, right):
        place = jnp.where(z < a, 0, 2) + zh
        return remote(at(k), fin.at[place], s3s.at[k], s3r.at[place], (left, right))

    def loop(fn):
        def step(k, carry):
            fn(k)
            return carry
        lax.fori_loop(0, 16, step, 0)

    def pair_send(late):
        def fn(k):
            z, s, left, right, used, early = block(k)

            @pl.when(used & (early != late) & (left % 2 != core))
            def _():
                pair_copy(k).start()
        loop(fn)

    def pair_sum(late):
        def fn(k):
            z, s, left, right, used, early = block(k)
            xp = (left // 2) % 4

            @pl.when(used & (early != late) & (left % 2 == core))
            def _():
                pair_copy(k).wait_recv()
                total = at(k)[...] + r1[k]

                @pl.when(xp == x)
                def _():
                    at(k)[...] = total

                @pl.when(xp != x)
                def _():
                    s2[k] = total.astype(BF)
                    x_copy(k, xp).start()
        loop(fn)

    def x_sum():
        def fn(k):
            z, s, left, right, used, early = block(k)
            xp = (left // 2) % 4

            @pl.when(used & (left % 2 == core) & (xp == x))
            def _():
                total = at(k)[...]
                for place in range(3):
                    remote(s2.at[k], r2.at[k, place], s2s.at[k], s2r.at[k, place], (r, c)).wait_recv()
                    total += r2[k, place].astype(F32)
                self = (left == r) & (right == c)

                @pl.when(self)
                def _():
                    fin[jnp.where(z < a, 0, 2) + zh] = total

                @pl.when(jnp.logical_not(self))
                def _():
                    at(k)[...] = total
                    last_copy(k, z, left, right).start()
        loop(fn)

    pair_send(False)
    pair_sum(False)

    y_lo_f.wait_recv()
    y_hi_f.wait_recv()
    fan_lo[2].wait_recv()
    turn_y(3)

    @pl.when(a == 3)
    def _():
        zu_cp[2].wait_recv()
        zt[2] = zu[2].T
        for s in (0, 1, 2):
            up(3, s)

    @pl.when(a == 0)
    def _():
        zd_cp[2].wait_recv()
        fan_hi[2].wait_recv()
        put(zd[2], 0, 0)
        apply(1, [(az, 3)])
        down(3, 0, 4)

    @pl.when(a > 0)
    def _():
        take_y(3, 0)
        apply(0, [(ap, 3)])

    for d in (1, 2, 3):
        @pl.when(a >= d)
        def _():
            up(d, 3)

    down(0, 3, 4)
    for d in (1, 2):
        @pl.when(a + d < 4)
        def _():
            down(d, 3, 4)

    pair_send(True)
    pair_sum(True)
    x_sum()

    zi, yi = r // 4, r % 4
    cross = zi < a
    plane = (zi == a) & (yi <= b)

    def fin_wait(place):
        remote(fin.at[place], fin.at[place], s3s.at[0], s3r.at[place], (r, c)).wait_recv()

    for place in range(4):
        if place < 2:
            needed = cross & jnp.logical_not((yi == b) & (zh == place))
        else:
            needed = cross | (plane & (zh != place - 2))

        @pl.when(needed)
        def _():
            fin_wait(place)

    @pl.when(cross)
    def _():
        out_ref[...] = (fin[0] + fin[1]) + (fin[2] + fin[3])

    @pl.when(plane)
    def _():
        out_ref[...] = fin[2] + fin[3]

    @pl.when(jnp.logical_not(cross | plane))
    def _():
        out_ref[...] = jnp.zeros_like(out_ref)

    for cp in [halo_up, halo_down, y_lo_n, y_hi_n, y_hi_p, y_lo_p, y_lo_f, y_hi_f] + fan_lo:
        cp.wait_send()
    for d in (1, 2, 3):
        @pl.when(a >= d)
        def _():
            fan_hi[d - 1].wait_send()

        @pl.when((a >= d - 1) & (a < 3))
        def _():
            zu_cp[d - 1].wait_send()

        @pl.when((a + d - 1 <= 3) & (a > 0))
        def _():
            zd_cp[d - 1].wait_send()

    def drain(k):
        z, s, left, right, used, early = block(k)
        xp = (left // 2) % 4

        @pl.when(used & (left % 2 != core))
        def _():
            pair_copy(k).wait_send()

        @pl.when(used & (left % 2 == core) & (xp != x))
        def _():
            x_copy(k, xp).wait_send()

        @pl.when(used & (left % 2 == core) & (xp == x) & jnp.logical_not((left == r) & (right == c)))
        def _():
            last_copy(k, z, left, right).wait_send()

    loop(drain)


def shards(basis, stiffness, block_cols, block_counts):
    dma = pltpu.SemaphoreType.DMA
    rows = jnp.arange(2 * NB, dtype=jnp.int32)
    first = lax.axis_index("row") * (2 * NB) - 2 + (rows // NB) * NB
    live = jnp.arange(CAP, dtype=jnp.int32)[None, :] < block_counts[:, None]
    idx = jnp.where(live, block_cols - first[:, None], DEAD)
    out = pl.pallas_call(
        kernel,
        out_shape=jax.ShapeDtypeStruct((PAN, 2 * PAN), F32),
        in_specs=[
            pl.BlockSpec(memory_space=pltpu.SMEM),
            pl.BlockSpec(memory_space=pltpu.HBM),
            pl.BlockSpec(memory_space=pltpu.HBM),
        ],
        out_specs=pl.BlockSpec(memory_space=pltpu.VMEM),
        scratch_shapes=[
            pltpu.VMEM((2, 2 * NB, BLOCK, CAP * BLOCK), BF),
            pltpu.VMEM((ROWS + 2 * HALO, PAN), BF),
            pltpu.VMEM((3, HALO + HALF, PAN), BF),
            pltpu.VMEM((3, HALF, PAN), BF),
            pltpu.VMEM((3, HALF, PAN), BF),
            pltpu.VMEM((3, EXT, PAN), BF),
            pltpu.VMEM((DEAD + 1, BLOCK, 2 * PAN), BF),
            pltpu.VMEM((2, 4 * PAN, HALF), BF),
            pltpu.VMEM((3, PAN, HALF), BF),
            pltpu.VMEM((4, HALF, 2 * PAN), BF),
            pltpu.VMEM((4, HALF, 2 * PAN), BF),
            pltpu.VMEM((4, 4 * PAN, 2 * PAN), F32),
            pltpu.VMEM((16, PAN, 2 * PAN), F32),
            pltpu.VMEM((16, PAN, 2 * PAN), BF),
            pltpu.VMEM((16, 3, PAN, 2 * PAN), BF),
            pltpu.VMEM((4, PAN, 2 * PAN), F32),
            dma((2,)), dma((2,)), dma((2,)), dma((6,)), dma((6,)), dma((6,)), dma((6,)),
            dma((3,)), dma((3,)), dma((3,)), dma((3,)),
            dma((16,)), dma((16,)), dma((16,)), dma((16, 3)), dma((16,)), dma((4,)),
        ],
        compiler_params=pltpu.CompilerParams(
            collective_id=0, has_side_effects=True, vmem_limit_bytes=56 * 2**20),
        cost_estimate=pl.CostEstimate(flops=8 * 10**9, bytes_accessed=10 * 2**20, transcendentals=0),
    )(idx.reshape(-1), basis, stiffness)
    return out.reshape(PAN, 2, PAN)


def solution(mesh):
    return jax.shard_map(
        shards,
        mesh=mesh,
        in_specs=(P("row", "col"), P(None, "row", None, None), P("row", None), P("row")),
        out_specs=P("row", None, "col"),
        check_vma=False,
    )
```

```python
import jax
import jax.numpy as jnp
from jax import lax
from jax.experimental import pallas as pl
from jax.experimental.pallas import tpu as pltpu
from jax.sharding import PartitionSpec as P

MESH = pl.DeviceIdType.MESH
BF = jnp.bfloat16
F32 = jnp.float32
BLOCK = 64
CAP = 8
HALO = 2 * BLOCK
ROWS = 4096
HALF = ROWS // 2
NB = HALF // BLOCK
EXT = HALF + 2 * HALO
DEAD = EXT // BLOCK
PAN = 128
UNROLL = 8
HC = PAN // 2
QC = HC // 4


def kernel(idx, basis_ref, stiff_ref, out_ref,
           sv, ox, ya, yh, zu, zd, g, pt, zt, ap, az, acc, r1, s2, r2, tot, fin,
           lsem, hs, hr, fs, fr, ys, yr, zus, zur, zds, zdr, s1s, s1r, s2s, s2r, s3s, s3r):
    r = lax.axis_index("row")
    c = lax.axis_index("col")
    core, x, zh = r % 2, (r // 2) % 4, r // 8
    a, b = c // 4, c % 4

    load_own = pltpu.make_async_copy(basis_ref, ox.at[pl.ds(HALO, ROWS)], lsem.at[0])
    load_own.start()
    load_s = pltpu.make_async_copy(stiff_ref, sv, lsem.at[1])
    load_s.start()

    def yb(d):
        return (b + d) % 4

    def ycol(d):
        return a * 4 + yb(d)

    def zcol(z):
        return z * 4 + b

    up_row, down_row = (r + 1) % 16, (r + 15) % 16
    barrier = pltpu.get_barrier_semaphore()

    def greet(i, carry):
        row = (r + i) % 16

        @pl.when(i > 0)
        def _():
            pl.semaphore_signal(barrier, inc=1, device_id=(row, c), device_id_type=MESH)

        for d in (1, 2, 3):
            pl.semaphore_signal(barrier, inc=1, device_id=(row, ycol(d)), device_id_type=MESH)
            pl.semaphore_signal(barrier, inc=1, device_id=(row, zcol((a + d) % 4)), device_id_type=MESH)
        return carry

    lax.fori_loop(0, 16, greet, 0)
    pl.semaphore_wait(barrier, 16 * 7 - 1)

    def remote(src, dst, ss, rs, dev):
        return pltpu.make_async_remote_copy(src_ref=src, dst_ref=dst, send_sem=ss, recv_sem=rs,
                                            device_id=dev, device_id_type=MESH)

    halo_up = remote(basis_ref.at[pl.ds(ROWS - HALO, HALO)], ox.at[pl.ds(0, HALO)], hs.at[0], hr.at[0], (up_row, c))
    halo_down = remote(basis_ref.at[pl.ds(0, HALO)], ox.at[pl.ds(ROWS + HALO, HALO)], hs.at[1], hr.at[1], (down_row, c))
    own_lo = basis_ref.at[pl.ds(0, HALF)]
    own_hi = basis_ref.at[pl.ds(HALF, HALF)]
    nxt, prv = (r, ycol(1)), (r, ycol(3))
    y_lo_n = remote(own_lo, ya.at[1, pl.ds(HALO, HALF)], ys.at[0], yr.at[0], nxt)
    y_hi_n = remote(own_hi, yh.at[1], ys.at[1], yr.at[1], nxt)
    y_hi_p = remote(own_hi, yh.at[0], ys.at[2], yr.at[2], prv)
    y_lo_p = remote(own_lo, ya.at[0, pl.ds(HALO, HALF)], ys.at[3], yr.at[3], prv)
    PIECE = HALF // 2
    y_lo_f = [remote(ya.at[1, pl.ds(HALO + p * PIECE, PIECE)], ya.at[2, pl.ds(HALO + p * PIECE, PIECE)],
                     ys.at[4 + p], yr.at[4 + p], nxt) for p in range(2)]
    y_hi_f = [remote(yh.at[0, pl.ds(p * PIECE, PIECE)], yh.at[2, pl.ds(p * PIECE, PIECE)],
                     ys.at[6 + p], yr.at[6 + p], prv) for p in range(2)]

    zup = (r, zcol((a + 1) % 4))
    zdn = (r, zcol((a + 3) % 4))
    DN = HALF + HALO
    UP_CUT = ((0, HALF // 2), (HALF // 2, HALF // 2))
    DN_CUT = ((0, HALF // 2 + BLOCK), (HALF // 2 + BLOCK, HALF // 2 + BLOCK))
    zu_cp, zd_cp = [], []
    for d in range(3):
        for p in range(2):
            o, n = UP_CUT[p]
            src = basis_ref.at[pl.ds(o, n)] if d == 0 else zu.at[d - 1, pl.ds(o, n)]
            zu_cp.append(remote(src, zu.at[d, pl.ds(o, n)], zus.at[2 * d + p], zur.at[2 * d + p], zup))
            o, n = DN_CUT[p]
            src = basis_ref.at[pl.ds(HALF - HALO + o, n)] if d == 0 else zd.at[d - 1, pl.ds(o, n)]
            zd_cp.append(remote(src, zd.at[d, pl.ds(o, n)], zds.at[2 * d + p], zdr.at[2 * d + p], zdn))

    for p in range(2):
        @pl.when(a < 3)
        def _():
            zu_cp[p].start()

        @pl.when(a > 0)
        def _():
            zd_cp[p].start()

    halo_up.start()
    halo_down.start()
    y_lo_n.start()
    y_hi_p.start()
    y_hi_n.start()
    y_lo_p.start()

    g[DEAD] = jnp.zeros((BLOCK, 2 * PAN), BF)

    halo_up.wait_recv()
    halo_down.wait_recv()
    fan_lo = [remote(ox.at[pl.ds(0, HALO)], ya.at[s - 1, pl.ds(0, HALO)], fs.at[s - 1], fr.at[s - 1], (r, ycol(dy)))
              for s, dy in ((1, 3), (2, 1), (3, 2))]
    fan_hi = [remote(ox.at[pl.ds(HALO + ROWS, HALO)], zd.at[d - 1, pl.ds(DN, HALO)], fs.at[2 + d], fr.at[2 + d],
                     (r, zcol((a + 4 - d) % 4))) for d in (1, 2, 3)]
    for cp in fan_lo:
        cp.start()
    for d in (1, 2, 3):
        @pl.when(a >= d)
        def _():
            fan_hi[d - 1].start()

    def apply(h, outs, lo=0, hi=NB):
        n = len(outs) * PAN

        def step(i, carry):
            row = h * NB + i
            lhs = jnp.concatenate([sv[0, row], sv[1, row]], axis=0)
            picked = jnp.concatenate(
                [g[idx[s, row]][:, 0:n] for s in range(CAP)], axis=0)
            res = jnp.dot(lhs, picked, preferred_element_type=F32).astype(BF)
            at = pl.ds(pl.multiple_of(i * BLOCK, BLOCK), BLOCK)
            for p, (ref, k) in enumerate(outs):
                for q in range(2):
                    ref[k, at, q * PAN:(q + 1) * PAN] = res[q * BLOCK:(q + 1) * BLOCK, p * PAN:(p + 1) * PAN]
            return carry

        lax.fori_loop(lo, hi, step, 0, unroll=UNROLL)

    def put(rows, at, lane):
        n = rows.shape[0] // BLOCK
        g[at:at + n, :, lane:lane + PAN] = rows.reshape(n, BLOCK, PAN)

    def take_y(s, lane):
        put(ya[s - 1], 0, lane)
        put(yh[s - 1, 0:HALO], DEAD - 2, lane)

    def turn_y(s, lo=0, hi=HALF):
        pt[0, s * PAN:(s + 1) * PAN, lo:hi] = ya[s - 1, HALO + lo:HALO + hi, :].T
        pt[1, s * PAN:(s + 1) * PAN, lo:hi] = yh[s - 1, lo:hi].T

    def keep(z, lo, res, more=False):
        for s in range(res.shape[0] // PAN):
            for half in range(2):
                at = s * PAN + half * HC
                rows = slice((lo + s) * HC, (lo + s + 1) * HC)
                if more:
                    acc[z, half, rows, :] += res[at:at + HC, :]
                else:
                    acc[z, half, rows, :] = res[at:at + HC, :]

    def down(d, lo, hi, k0=0, k1=HALF):
        res = jnp.dot(pt[1, lo * PAN:hi * PAN, k0:k1], az[d, k0:k1, :], preferred_element_type=F32)
        if d == 0:
            res += jnp.dot(pt[0, lo * PAN:hi * PAN, k0:k1], ap[0, k0:k1, :], preferred_element_type=F32)
        keep(a + d, lo, res, k0 > 0)

    def up(d, s, k0=0, k1=HALF):
        keep(a - d, s, jnp.dot(zt[d - 1, :, k0:k1], ap[s, k0:k1, :], preferred_element_type=F32), k0 > 0)

    def pass_on(d):
        for p in range(2 * d, 2 * d + 2):
            @pl.when(a > d)
            def _():
                zu_cp[p].wait_recv()

            @pl.when((a > d) & (a < 3))
            def _():
                zu_cp[p + 2].start()

            @pl.when(a + d < 3)
            def _():
                zd_cp[p].wait_recv()

            @pl.when((a + d < 3) & (a > 0))
            def _():
                zd_cp[p + 2].start()

    load_own.wait()
    load_s.wait()
    put(ox[0:EXT, :], 0, 0)
    apply(0, [(ap, 0)])
    pt[0, 0:PAN, :] = ox[HALO:HALO + HALF, :].T
    pt[1, 0:PAN, :] = ox[HALO + HALF:HALO + ROWS, :].T

    pass_on(0)

    y_lo_n.wait_recv()
    y_hi_p.wait_recv()
    for p in range(2):
        y_lo_f[p].start()
        y_hi_f[p].start()

    put(ox[HALF:HALF + EXT, :], 0, 0)

    @pl.when(a < 3)
    def _():
        fan_hi[0].wait_recv()
        put(zd[0], 0, PAN)
        apply(1, [(az, 0), (az, 1)])

    @pl.when(a == 3)
    def _():
        apply(1, [(az, 0)])

    pass_on(1)
    y_hi_n.wait_recv()
    y_lo_p.wait_recv()
    for s in (1, 2):
        fan_lo[s - 1].wait_recv()
        turn_y(s)

    @pl.when(a > 0)
    def _():
        take_y(1, 0)
        take_y(2, PAN)
        apply(0, [(ap, 1), (ap, 2)])
        zt[0] = zu[0].T
        for s in (0, 1, 2):
            up(1, s)

    @pl.when(a > 1)
    def _():
        zt[1] = zu[1].T
        for s in (0, 1, 2):
            up(2, s)

    down(0, 0, 3)

    @pl.when(a < 3)
    def _():
        down(1, 0, 3)

    @pl.when(a < 2)
    def _():
        fan_hi[1].wait_recv()
        put(zd[1], 0, 0)
        apply(1, [(az, 2)])
        down(2, 0, 3)

    EARLY, LATE = (0, 3), (3, 4)

    def each(fn, which):
        def step(z, carry):
            far = (z - a == 3) | (a - z == 3)
            if which == "early":
                @pl.when(jnp.logical_not(far))
                def _():
                    fn(z, 0, *EARLY)
            elif which == "late":
                @pl.when(far)
                def _():
                    fn(z, 0, *EARLY)
                fn(z, 1, *LATE)
            else:
                fn(z, 0, *EARLY)
                fn(z, 1, *LATE)
            return carry
        lax.fori_loop(0, 4, step, 0)

    def pair_copy(z, w, lo, hi):
        rows = pl.ds(lo * HC, (hi - lo) * HC)
        return remote(acc.at[z, 1 - core, rows], r1.at[z, rows], s1s.at[z, w], s1r.at[z, w],
                      (zh * 8 + x * 2 + (1 - core), c))

    def x_copy(z, w, lo, hi, d):
        rows = pl.ds(lo * QC, (hi - lo) * QC)
        return remote(s2.at[z, d - 1, rows], r2.at[z, d - 1, rows], s2s.at[z, w, d - 1], s2r.at[z, w, d - 1],
                      (zh * 8 + ((x + d) % 4) * 2 + core, c))

    def owner(z, s):
        y = (b + s + (s // 2) * (1 - 2 * (s % 2))) % 4
        left = jnp.where(z < a, z * 4 + b, a * 4 + y)
        right = jnp.where(z < a, a * 4 + y, z * 4 + b)
        place = jnp.where(z < a, 0, 2) + zh
        return left, right, place, (z != a) | (y <= b)

    share = pl.ds(pl.multiple_of(core * HC + x * QC, QC), QC)

    def last_copy(z, s, left, right, place):
        return remote(tot.at[z, s], fin.at[place, share], s3s.at[z, s], s3r.at[place], (left, right))

    def pair_send(z, w, lo, hi):
        pair_copy(z, w, lo, hi).start()

    def pair_sum(z, w, lo, hi):
        pair_copy(z, w, lo, hi).wait_recv()
        for s in range(lo, hi):
            for d in (1, 2, 3):
                rows = pl.ds(pl.multiple_of(s * HC + ((x + d) % 4) * QC, QC), QC)
                s2[z, d - 1, s * QC:(s + 1) * QC, :] = (acc[z, core, rows, :] + r1[z, rows, :]).astype(BF)
        for d in (1, 2, 3):
            x_copy(z, w, lo, hi, d).start()

    def x_sum(z, w, lo, hi):
        for d in (1, 2, 3):
            x_copy(z, w, lo, hi, d).wait_recv()
        for s in range(lo, hi):
            rows = pl.ds(pl.multiple_of(s * HC + x * QC, QC), QC)
            part = acc[z, core, rows, :] + r1[z, rows, :]
            for d in (1, 2, 3):
                part += r2[z, d - 1, s * QC:(s + 1) * QC, :].astype(F32)
            left, right, place, used = owner(z, s)
            here = (left == r) & (right == c)

            @pl.when(used & here)
            def _():
                fin[place, share, :] = part

            @pl.when(used & jnp.logical_not(here))
            def _():
                tot[z, s] = part
                last_copy(z, s, left, right, place).start()

    each(pair_send, "early")
    each(pair_sum, "early")

    E0 = HALO + PIECE
    N0 = E0 // BLOCK - 4
    READY = DN_CUT[0][1] // BLOCK - 5
    for p in range(2):
        lo, hi = p * PIECE, (p + 1) * PIECE
        y_lo_f[p].wait_recv()
        y_hi_f[p].wait_recv()
        if p == 0:
            fan_lo[2].wait_recv()
        turn_y(3, lo, hi)

        @pl.when(a == 3)
        def _():
            zu_cp[4 + p].wait_recv()
            zt[2, :, lo:hi] = zu[2, lo:hi].T
            for s in (0, 1, 2):
                up(3, s, lo, hi)

        @pl.when(a == 0)
        def _():
            zd_cp[4 + p].wait_recv()
            o, n = DN_CUT[p]
            put(zd[2, o:o + n], o // BLOCK, 0)
            if p == 0:
                apply(1, [(az, 3)], 0, READY)
                down(3, 0, 3, 0, READY * BLOCK)
            else:
                fan_hi[2].wait_recv()
                put(zd[2, DN:EXT], DEAD - 2, 0)
                apply(1, [(az, 3)], READY, NB)
                down(3, 0, 3, READY * BLOCK, HALF)
                down(3, 3, 4)

        @pl.when(a > 0)
        def _():
            if p == 0:
                put(ya[2, 0:E0], 0, 0)
                apply(0, [(ap, 3)], 0, N0)
            else:
                put(ya[2, E0:HALO + HALF], E0 // BLOCK, 0)
                put(yh[2, 0:HALO], DEAD - 2, 0)
                apply(0, [(ap, 3)], N0, NB)

        for d in (1, 2, 3):
            @pl.when(a >= d)
            def _():
                if p == 0:
                    up(d, 3, 0, N0 * BLOCK)
                else:
                    up(d, 3, N0 * BLOCK, HALF)

        down(0, 3, 4, lo, hi)
        for d in (1, 2):
            @pl.when(a + d < 4)
            def _():
                down(d, 3, 4, lo, hi)

        if p == 0:
            each(x_sum, "early")

    each(pair_send, "late")
    each(pair_sum, "late")
    each(x_sum, "late")

    zi, yi = r // 4, r % 4
    cross = zi < a
    plane = (zi == a) & (yi <= b)

    def fin_wait(place, rows):
        part = fin.at[place, pl.ds(0, rows)]
        remote(part, part, s3s.at[0, 0], s3r.at[place], (r, other)).wait_recv()

    other = ycol(1)
    for place in range(4):
        if place < 2:
            wanted, here = cross, (yi == b) & (zh == place)
        else:
            wanted, here = cross | plane, plane & (zh == place - 2)

        @pl.when(wanted & here)
        def _():
            fin_wait(place, PAN - QC)

        @pl.when(wanted & jnp.logical_not(here))
        def _():
            fin_wait(place, PAN)

    @pl.when(cross)
    def _():
        out_ref[...] = (fin[0] + fin[1]) + (fin[2] + fin[3])

    @pl.when(plane)
    def _():
        out_ref[...] = fin[2] + fin[3]

    @pl.when(jnp.logical_not(cross | plane))
    def _():
        out_ref[...] = jnp.zeros_like(out_ref)

    for cp in [halo_up, halo_down, y_lo_n, y_hi_n, y_hi_p, y_lo_p] + y_lo_f + y_hi_f + fan_lo:
        cp.wait_send()
    for d in (1, 2, 3):
        @pl.when(a >= d)
        def _():
            fan_hi[d - 1].wait_send()

        @pl.when((a >= d - 1) & (a < 3))
        def _():
            zu_cp[2 * d - 2].wait_send()
            zu_cp[2 * d - 1].wait_send()

        @pl.when((a + d - 1 <= 3) & (a > 0))
        def _():
            zd_cp[2 * d - 2].wait_send()
            zd_cp[2 * d - 1].wait_send()

    def drain(z, w, lo, hi):
        pair_copy(z, w, lo, hi).wait_send()
        for d in (1, 2, 3):
            x_copy(z, w, lo, hi, d).wait_send()
        for s in range(lo, hi):
            left, right, place, used = owner(z, s)

            @pl.when(used & jnp.logical_not((left == r) & (right == c)))
            def _():
                last_copy(z, s, left, right, place).wait_send()

    each(drain, "all")


def shards(basis, stiffness, block_cols, block_counts):
    dma = pltpu.SemaphoreType.DMA
    rows = jnp.arange(2 * NB, dtype=jnp.int32)
    first = lax.axis_index("row") * (2 * NB) - 2 + (rows // NB) * NB
    live = jnp.arange(CAP, dtype=jnp.int32)[:, None] < block_counts[None, :]
    idx = jnp.where(live, block_cols.T - first[None, :], DEAD)
    out = pl.pallas_call(
        kernel,
        out_shape=jax.ShapeDtypeStruct((PAN, 2 * PAN), F32),
        in_specs=[
            pl.BlockSpec(memory_space=pltpu.SMEM),
            pl.BlockSpec(memory_space=pltpu.HBM),
            pl.BlockSpec(memory_space=pltpu.HBM),
        ],
        out_specs=pl.BlockSpec(memory_space=pltpu.VMEM),
        scratch_shapes=[
            pltpu.VMEM((2, 2 * NB, BLOCK, CAP * BLOCK), BF),
            pltpu.VMEM((ROWS + 2 * HALO, PAN), BF),
            pltpu.VMEM((3, HALO + HALF, PAN), BF),
            pltpu.VMEM((3, HALF, PAN), BF),
            pltpu.VMEM((3, HALF, PAN), BF),
            pltpu.VMEM((3, EXT, PAN), BF),
            pltpu.VMEM((DEAD + 1, BLOCK, 2 * PAN), BF),
            pltpu.VMEM((2, 4 * PAN, HALF), BF),
            pltpu.VMEM((3, PAN, HALF), BF),
            pltpu.VMEM((4, HALF, 2 * PAN), BF),
            pltpu.VMEM((4, HALF, 2 * PAN), BF),
            pltpu.VMEM((4, 2, 4 * HC, 2 * PAN), F32),
            pltpu.VMEM((4, 4 * HC, 2 * PAN), F32),
            pltpu.VMEM((4, 3, 4 * QC, 2 * PAN), BF),
            pltpu.VMEM((4, 3, 4 * QC, 2 * PAN), BF),
            pltpu.VMEM((4, 4, QC, 2 * PAN), F32),
            pltpu.VMEM((4, PAN, 2 * PAN), F32),
            dma((2,)), dma((2,)), dma((2,)), dma((6,)), dma((6,)), dma((8,)), dma((8,)),
            dma((6,)), dma((6,)), dma((6,)), dma((6,)),
            dma((4, 2)), dma((4, 2)), dma((4, 2, 3)), dma((4, 2, 3)), dma((4, 4)), dma((4,)),
        ],
        compiler_params=pltpu.CompilerParams(
            collective_id=0, has_side_effects=True, vmem_limit_bytes=56 * 2**20),
        cost_estimate=pl.CostEstimate(flops=8 * 10**9, bytes_accessed=10 * 2**20, transcendentals=0),
    )(idx, basis, stiffness)
    return out.reshape(PAN, 2, PAN)


def solution(mesh):
    return jax.shard_map(
        shards,
        mesh=mesh,
        in_specs=(P("row", "col"), P(None, "row", None, None), P("row", None), P("row")),
        out_specs=P("row", None, "col"),
        check_vma=False,
    )
```

```python
import jax
import jax.numpy as jnp
from jax import lax
from jax.experimental import pallas as pl
from jax.experimental.pallas import tpu as pltpu
from jax.sharding import PartitionSpec as P

MESH = pl.DeviceIdType.MESH
BF = jnp.bfloat16
F32 = jnp.float32
BLOCK = 64
CAP = 8
HALO = 2 * BLOCK
ROWS = 4096
HALF = ROWS // 2
NB = HALF // BLOCK
EXT = HALF + 2 * HALO
DEAD = EXT // BLOCK
PAN = 128
UNROLL = 8
HC = PAN // 2
QC = HC // 4


def kernel(cols_ref, counts_ref, basis_ref, stiff_ref, out_ref,
           sv, ox, ya, yh, zu, zd, g, pt, zt, ap, az, acc, r1, s2, r2, tot, fin,
           lsem, hs, hr, fs, fr, ys, yr, zus, zur, zds, zdr, s1s, s1r, s2s, s2r, s3s, s3r):
    r = lax.axis_index("row")
    c = lax.axis_index("col")
    core, x, zh = r % 2, (r // 2) % 4, r // 8
    a, b = c // 4, c % 4

    load_own = pltpu.make_async_copy(basis_ref, ox.at[pl.ds(HALO, ROWS)], lsem.at[0])
    load_own.start()
    load_s = pltpu.make_async_copy(stiff_ref, sv, lsem.at[1])
    load_s.start()

    def yb(d):
        return (b + d) % 4

    def ycol(d):
        return a * 4 + yb(d)

    def zcol(z):
        return z * 4 + b

    up_row, down_row = (r + 1) % 16, (r + 15) % 16
    barrier = pltpu.get_barrier_semaphore()

    def greet(i, carry):
        row = (r + i) % 16

        @pl.when(i > 0)
        def _():
            pl.semaphore_signal(barrier, inc=1, device_id=(row, c), device_id_type=MESH)

        for d in (1, 2, 3):
            pl.semaphore_signal(barrier, inc=1, device_id=(row, ycol(d)), device_id_type=MESH)
            pl.semaphore_signal(barrier, inc=1, device_id=(row, zcol((a + d) % 4)), device_id_type=MESH)
        return carry

    lax.fori_loop(0, 16, greet, 0)
    pl.semaphore_wait(barrier, 16 * 7 - 1)

    def remote(src, dst, ss, rs, dev):
        return pltpu.make_async_remote_copy(src_ref=src, dst_ref=dst, send_sem=ss, recv_sem=rs,
                                            device_id=dev, device_id_type=MESH)

    halo_up = remote(basis_ref.at[pl.ds(ROWS - HALO, HALO)], ox.at[pl.ds(0, HALO)], hs.at[0], hr.at[0], (up_row, c))
    halo_down = remote(basis_ref.at[pl.ds(0, HALO)], ox.at[pl.ds(ROWS + HALO, HALO)], hs.at[1], hr.at[1], (down_row, c))
    own_lo = basis_ref.at[pl.ds(0, HALF)]
    own_hi = basis_ref.at[pl.ds(HALF, HALF)]
    nxt, prv = (r, ycol(1)), (r, ycol(3))
    y_lo_n = remote(own_lo, ya.at[1, pl.ds(HALO, HALF)], ys.at[0], yr.at[0], nxt)
    y_hi_n = remote(own_hi, yh.at[1], ys.at[1], yr.at[1], nxt)
    y_hi_p = remote(own_hi, yh.at[0], ys.at[2], yr.at[2], prv)
    y_lo_p = remote(own_lo, ya.at[0, pl.ds(HALO, HALF)], ys.at[3], yr.at[3], prv)
    PIECE = HALF // 2
    y_lo_f = [remote(ya.at[1, pl.ds(HALO + p * PIECE, PIECE)], ya.at[2, pl.ds(HALO + p * PIECE, PIECE)],
                     ys.at[4 + p], yr.at[4 + p], nxt) for p in range(2)]
    y_hi_f = [remote(yh.at[0, pl.ds(p * PIECE, PIECE)], yh.at[2, pl.ds(p * PIECE, PIECE)],
                     ys.at[6 + p], yr.at[6 + p], prv) for p in range(2)]

    zup = (r, zcol((a + 1) % 4))
    zdn = (r, zcol((a + 3) % 4))
    DN = HALF + HALO
    UP_CUT = ((0, HALF // 2), (HALF // 2, HALF // 2))
    DN_CUT = ((0, HALF // 2 + BLOCK), (HALF // 2 + BLOCK, HALF // 2 + BLOCK))
    zu_cp, zd_cp = [], []
    for d in range(3):
        for p in range(2):
            o, n = UP_CUT[p]
            src = basis_ref.at[pl.ds(o, n)] if d == 0 else zu.at[d - 1, pl.ds(o, n)]
            zu_cp.append(remote(src, zu.at[d, pl.ds(o, n)], zus.at[2 * d + p], zur.at[2 * d + p], zup))
            o, n = DN_CUT[p]
            src = basis_ref.at[pl.ds(HALF - HALO + o, n)] if d == 0 else zd.at[d - 1, pl.ds(o, n)]
            zd_cp.append(remote(src, zd.at[d, pl.ds(o, n)], zds.at[2 * d + p], zdr.at[2 * d + p], zdn))

    for p in range(2):
        @pl.when(a < 3)
        def _():
            zu_cp[p].start()

        @pl.when(a > 0)
        def _():
            zd_cp[p].start()

    halo_up.start()
    halo_down.start()
    y_lo_n.start()
    y_hi_p.start()
    y_hi_n.start()
    y_lo_p.start()

    g[DEAD] = jnp.zeros((BLOCK, 2 * PAN), BF)

    halo_up.wait_recv()
    halo_down.wait_recv()
    fan_lo = [remote(ox.at[pl.ds(0, HALO)], ya.at[s - 1, pl.ds(0, HALO)], fs.at[s - 1], fr.at[s - 1], (r, ycol(dy)))
              for s, dy in ((1, 3), (2, 1), (3, 2))]
    fan_hi = [remote(ox.at[pl.ds(HALO + ROWS, HALO)], zd.at[d - 1, pl.ds(DN, HALO)], fs.at[2 + d], fr.at[2 + d],
                     (r, zcol((a + 4 - d) % 4))) for d in (1, 2, 3)]
    for cp in fan_lo:
        cp.start()
    for d in (1, 2, 3):
        @pl.when(a >= d)
        def _():
            fan_hi[d - 1].start()

    def apply(h, outs, lo=0, hi=NB):
        n = len(outs) * PAN

        def step(i, carry):
            row = h * NB + i
            lhs = jnp.concatenate([sv[0, row], sv[1, row]], axis=0)
            first = r * (2 * NB) + h * NB - 2
            picks = [i + 2] + [jnp.clip(cols_ref[s, row] - first, 0, DEAD) for s in range(1, CAP)]
            for s in range(3, CAP):
                picks[s] = jnp.where(s < counts_ref[row], picks[s], DEAD)
            picked = jnp.concatenate([g[k][:, 0:n] for k in picks], axis=0)
            res = jnp.dot(lhs, picked, preferred_element_type=F32).astype(BF)
            at = pl.ds(pl.multiple_of(i * BLOCK, BLOCK), BLOCK)
            for p, (ref, k) in enumerate(outs):
                for q in range(2):
                    ref[k, at, q * PAN:(q + 1) * PAN] = res[q * BLOCK:(q + 1) * BLOCK, p * PAN:(p + 1) * PAN]
            return carry

        lax.fori_loop(lo, hi, step, 0, unroll=UNROLL)

    def put(rows, at, lane):
        n = rows.shape[0] // BLOCK
        g[at:at + n, :, lane:lane + PAN] = rows.reshape(n, BLOCK, PAN)

    def take_y(s, lane):
        put(ya[s - 1], 0, lane)
        put(yh[s - 1, 0:HALO], DEAD - 2, lane)

    def turn_y(s, lo=0, hi=HALF):
        pt[0, s * PAN:(s + 1) * PAN, lo:hi] = ya[s - 1, HALO + lo:HALO + hi, :].T
        pt[1, s * PAN:(s + 1) * PAN, lo:hi] = yh[s - 1, lo:hi].T

    def keep(z, lo, res, more=False):
        for s in range(res.shape[0] // PAN):
            for half in range(2):
                at = s * PAN + half * HC
                rows = slice((lo + s) * HC, (lo + s + 1) * HC)
                if more:
                    acc[z, half, rows, :] += res[at:at + HC, :]
                else:
                    acc[z, half, rows, :] = res[at:at + HC, :]

    def down(d, lo, hi, k0=0, k1=HALF):
        res = jnp.dot(pt[1, lo * PAN:hi * PAN, k0:k1], az[d, k0:k1, :], preferred_element_type=F32)
        if d == 0:
            res += jnp.dot(pt[0, lo * PAN:hi * PAN, k0:k1], ap[0, k0:k1, :], preferred_element_type=F32)
        keep(a + d, lo, res, k0 > 0)

    def up(d, s, k0=0, k1=HALF):
        keep(a - d, s, jnp.dot(zt[d - 1, :, k0:k1], ap[s, k0:k1, :], preferred_element_type=F32), k0 > 0)

    def pass_on(d):
        for p in range(2 * d, 2 * d + 2):
            @pl.when(a > d)
            def _():
                zu_cp[p].wait_recv()

            @pl.when((a > d) & (a < 3))
            def _():
                zu_cp[p + 2].start()

            @pl.when(a + d < 3)
            def _():
                zd_cp[p].wait_recv()

            @pl.when((a + d < 3) & (a > 0))
            def _():
                zd_cp[p + 2].start()

    load_own.wait()
    load_s.wait()
    put(ox[0:EXT, :], 0, 0)
    apply(0, [(ap, 0)])
    pt[0, 0:PAN, :] = ox[HALO:HALO + HALF, :].T
    pt[1, 0:PAN, :] = ox[HALO + HALF:HALO + ROWS, :].T

    pass_on(0)

    y_lo_n.wait_recv()
    y_hi_p.wait_recv()
    for p in range(2):
        y_lo_f[p].start()
        y_hi_f[p].start()

    put(ox[HALF:HALF + EXT, :], 0, 0)

    @pl.when(a < 3)
    def _():
        fan_hi[0].wait_recv()
        put(zd[0], 0, PAN)
        apply(1, [(az, 0), (az, 1)])

    @pl.when(a == 3)
    def _():
        apply(1, [(az, 0)])

    down(0, 0, 1)

    @pl.when(a < 3)
    def _():
        down(1, 0, 1)

    @pl.when(a > 0)
    def _():
        zt[0] = zu[0].T
        up(1, 0)

    pass_on(1)
    y_hi_n.wait_recv()
    y_lo_p.wait_recv()
    for s in (1, 2):
        fan_lo[s - 1].wait_recv()
        turn_y(s)

    @pl.when(a > 0)
    def _():
        take_y(1, 0)
        take_y(2, PAN)
        apply(0, [(ap, 1), (ap, 2)])
        for s in (1, 2):
            up(1, s)

    @pl.when(a > 1)
    def _():
        zt[1] = zu[1].T
        for s in (0, 1, 2):
            up(2, s)

    down(0, 1, 3)

    @pl.when(a < 3)
    def _():
        down(1, 1, 3)

    @pl.when(a < 2)
    def _():
        fan_hi[1].wait_recv()
        put(zd[1], 0, 0)
        apply(1, [(az, 2)])
        down(2, 0, 3)

    EARLY, LATE = (0, 3), (3, 4)

    def each(fn, which):
        def step(z, carry):
            far = (z - a == 3) | (a - z == 3)
            if which == "early":
                @pl.when(jnp.logical_not(far))
                def _():
                    fn(z, 0, *EARLY)
            elif which == "late":
                @pl.when(far)
                def _():
                    fn(z, 0, *EARLY)
                fn(z, 1, *LATE)
            else:
                fn(z, 0, *EARLY)
                fn(z, 1, *LATE)
            return carry
        lax.fori_loop(0, 4, step, 0)

    def pair_copy(z, w, lo, hi):
        rows = pl.ds(lo * HC, (hi - lo) * HC)
        return remote(acc.at[z, 1 - core, rows], r1.at[z, rows], s1s.at[z, w], s1r.at[z, w],
                      (zh * 8 + x * 2 + (1 - core), c))

    def x_copy(z, w, lo, hi, d):
        rows = pl.ds(lo * QC, (hi - lo) * QC)
        return remote(s2.at[z, d - 1, rows], r2.at[z, d - 1, rows], s2s.at[z, w, d - 1], s2r.at[z, w, d - 1],
                      (zh * 8 + ((x + d) % 4) * 2 + core, c))

    def owner(z, s):
        y = (b + s + (s // 2) * (1 - 2 * (s % 2))) % 4
        left = jnp.where(z < a, z * 4 + b, a * 4 + y)
        right = jnp.where(z < a, a * 4 + y, z * 4 + b)
        place = jnp.where(z < a, 0, 2) + zh
        return left, right, place, (z != a) | (y <= b)

    share = pl.ds(pl.multiple_of(core * HC + x * QC, QC), QC)

    def last_copy(z, s, left, right, place):
        return remote(tot.at[z, s], fin.at[place, share], s3s.at[z, s], s3r.at[place], (left, right))

    def pair_send(z, w, lo, hi):
        pair_copy(z, w, lo, hi).start()

    def pair_sum(z, w, lo, hi):
        pair_copy(z, w, lo, hi).wait_recv()
        for s in range(lo, hi):
            for d in (1, 2, 3):
                rows = pl.ds(pl.multiple_of(s * HC + ((x + d) % 4) * QC, QC), QC)
                s2[z, d - 1, s * QC:(s + 1) * QC, :] = (acc[z, core, rows, :] + r1[z, rows, :]).astype(BF)
        for d in (1, 2, 3):
            x_copy(z, w, lo, hi, d).start()

    def x_sum(z, w, lo, hi):
        for d in (1, 2, 3):
            x_copy(z, w, lo, hi, d).wait_recv()
        for s in range(lo, hi):
            rows = pl.ds(pl.multiple_of(s * HC + x * QC, QC), QC)
            part = acc[z, core, rows, :] + r1[z, rows, :]
            for d in (1, 2, 3):
                part += r2[z, d - 1, s * QC:(s + 1) * QC, :].astype(F32)
            left, right, place, used = owner(z, s)
            here = (left == r) & (right == c)

            @pl.when(used & here)
            def _():
                fin[place, share, :] = part.astype(BF)

            @pl.when(used & jnp.logical_not(here))
            def _():
                tot[z, s] = part.astype(BF)
                last_copy(z, s, left, right, place).start()

    each(pair_send, "early")

    E0 = HALO + PIECE
    N0 = E0 // BLOCK - 4
    READY = DN_CUT[0][1] // BLOCK - 5
    for p in range(2):
        lo, hi = p * PIECE, (p + 1) * PIECE
        y_lo_f[p].wait_recv()
        y_hi_f[p].wait_recv()
        if p == 0:
            fan_lo[2].wait_recv()
        turn_y(3, lo, hi)

        @pl.when(a == 3)
        def _():
            zu_cp[4 + p].wait_recv()
            zt[2, :, lo:hi] = zu[2, lo:hi].T
            for s in (0, 1, 2):
                up(3, s, lo, hi)

        @pl.when(a == 0)
        def _():
            zd_cp[4 + p].wait_recv()
            o, n = DN_CUT[p]
            put(zd[2, o:o + n], o // BLOCK, 0)
            if p == 0:
                apply(1, [(az, 3)], 0, READY)
                down(3, 0, 3, 0, READY * BLOCK)
            else:
                fan_hi[2].wait_recv()
                put(zd[2, DN:EXT], DEAD - 2, 0)
                apply(1, [(az, 3)], READY, NB)
                down(3, 0, 3, READY * BLOCK, HALF)
                down(3, 3, 4)

        @pl.when(a > 0)
        def _():
            if p == 0:
                put(ya[2, 0:E0], 0, 0)
                apply(0, [(ap, 3)], 0, N0)
            else:
                put(ya[2, E0:HALO + HALF], E0 // BLOCK, 0)
                put(yh[2, 0:HALO], DEAD - 2, 0)
                apply(0, [(ap, 3)], N0, NB)

        for d in (1, 2, 3):
            @pl.when(a >= d)
            def _():
                if p == 0:
                    up(d, 3, 0, N0 * BLOCK)
                else:
                    up(d, 3, N0 * BLOCK, HALF)

        down(0, 3, 4, lo, hi)
        for d in (1, 2):
            @pl.when(a + d < 4)
            def _():
                down(d, 3, 4, lo, hi)

        if p == 0:
            each(pair_sum, "early")

    each(pair_send, "late")
    each(x_sum, "early")
    each(pair_sum, "late")
    each(x_sum, "late")

    zi, yi = r // 4, r % 4
    cross = zi < a
    plane = (zi == a) & (yi <= b)

    def fin_wait(place, rows):
        part = fin.at[place, pl.ds(0, rows)]
        remote(part, part, s3s.at[0, 0], s3r.at[place], (r, other)).wait_recv()

    other = ycol(1)
    for place in range(4):
        if place < 2:
            wanted, here = cross, (yi == b) & (zh == place)
        else:
            wanted, here = cross | plane, plane & (zh == place - 2)

        @pl.when(wanted & here)
        def _():
            fin_wait(place, PAN - QC)

        @pl.when(wanted & jnp.logical_not(here))
        def _():
            fin_wait(place, PAN)

    @pl.when(cross)
    def _():
        out_ref[...] = (fin[0].astype(F32) + fin[1].astype(F32)) + (fin[2].astype(F32) + fin[3].astype(F32))

    @pl.when(plane)
    def _():
        out_ref[...] = fin[2].astype(F32) + fin[3].astype(F32)

    @pl.when(jnp.logical_not(cross | plane))
    def _():
        out_ref[...] = jnp.zeros_like(out_ref)

    for cp in [halo_up, halo_down, y_lo_n, y_hi_n, y_hi_p, y_lo_p] + y_lo_f + y_hi_f + fan_lo:
        cp.wait_send()
    for d in (1, 2, 3):
        @pl.when(a >= d)
        def _():
            fan_hi[d - 1].wait_send()

        @pl.when((a >= d - 1) & (a < 3))
        def _():
            zu_cp[2 * d - 2].wait_send()
            zu_cp[2 * d - 1].wait_send()

        @pl.when((a + d - 1 <= 3) & (a > 0))
        def _():
            zd_cp[2 * d - 2].wait_send()
            zd_cp[2 * d - 1].wait_send()

    def drain(z, w, lo, hi):
        pair_copy(z, w, lo, hi).wait_send()
        for d in (1, 2, 3):
            x_copy(z, w, lo, hi, d).wait_send()
        for s in range(lo, hi):
            left, right, place, used = owner(z, s)

            @pl.when(used & jnp.logical_not((left == r) & (right == c)))
            def _():
                last_copy(z, s, left, right, place).wait_send()

    each(drain, "all")


def shards(basis, stiffness, block_cols, block_counts):
    dma = pltpu.SemaphoreType.DMA
    out = pl.pallas_call(
        kernel,
        out_shape=jax.ShapeDtypeStruct((PAN, 2 * PAN), F32),
        in_specs=[
            pl.BlockSpec(memory_space=pltpu.SMEM),
            pl.BlockSpec(memory_space=pltpu.SMEM),
            pl.BlockSpec(memory_space=pltpu.HBM),
            pl.BlockSpec(memory_space=pltpu.HBM),
        ],
        out_specs=pl.BlockSpec(memory_space=pltpu.VMEM),
        scratch_shapes=[
            pltpu.VMEM((2, 2 * NB, BLOCK, CAP * BLOCK), BF),
            pltpu.VMEM((ROWS + 2 * HALO, PAN), BF),
            pltpu.VMEM((3, HALO + HALF, PAN), BF),
            pltpu.VMEM((3, HALF, PAN), BF),
            pltpu.VMEM((3, HALF, PAN), BF),
            pltpu.VMEM((3, EXT, PAN), BF),
            pltpu.VMEM((DEAD + 1, BLOCK, 2 * PAN), BF),
            pltpu.VMEM((2, 4 * PAN, HALF), BF),
            pltpu.VMEM((3, PAN, HALF), BF),
            pltpu.VMEM((4, HALF, 2 * PAN), BF),
            pltpu.VMEM((4, HALF, 2 * PAN), BF),
            pltpu.VMEM((4, 2, 4 * HC, 2 * PAN), F32),
            pltpu.VMEM((4, 4 * HC, 2 * PAN), F32),
            pltpu.VMEM((4, 3, 4 * QC, 2 * PAN), BF),
            pltpu.VMEM((4, 3, 4 * QC, 2 * PAN), BF),
            pltpu.VMEM((4, 4, QC, 2 * PAN), BF),
            pltpu.VMEM((4, PAN, 2 * PAN), BF),
            dma((2,)), dma((2,)), dma((2,)), dma((6,)), dma((6,)), dma((8,)), dma((8,)),
            dma((6,)), dma((6,)), dma((6,)), dma((6,)),
            dma((4, 2)), dma((4, 2)), dma((4, 2, 3)), dma((4, 2, 3)), dma((4, 4)), dma((4,)),
        ],
        compiler_params=pltpu.CompilerParams(
            collective_id=0, has_side_effects=True, vmem_limit_bytes=56 * 2**20),
        cost_estimate=pl.CostEstimate(flops=8 * 10**9, bytes_accessed=10 * 2**20, transcendentals=0),
    )(block_cols.T, block_counts, basis, stiffness)
    return out.reshape(PAN, 2, PAN)


def solution(mesh):
    return jax.shard_map(
        shards,
        mesh=mesh,
        in_specs=(P("row", "col"), P(None, "row", None, None), P("row", None), P("row")),
        out_specs=P("row", None, "col"),
        check_vma=False,
    )
```

```python
import jax
import jax.numpy as jnp
from jax import lax
from jax.experimental import pallas as pl
from jax.experimental.pallas import tpu as pltpu
from jax.sharding import PartitionSpec as P

MESH = pl.DeviceIdType.MESH
BF = jnp.bfloat16
F32 = jnp.float32
BLOCK = 64
CAP = 8
HALO = 2 * BLOCK
ROWS = 4096
HALF = ROWS // 2
NB = HALF // BLOCK
EXT = HALF + 2 * HALO
DEAD = EXT // BLOCK
PAN = 128
UNROLL = 8
HC = PAN // 2
QC = HC // 4


def kernel(cols_ref, counts_ref, basis_ref, stiff_ref, out_ref,
           sv, ox, ya, yh, zu, zd, g, pt, zt, ap, az, acc, r1, s2, r2, tot, fin,
           lsem, hs, hr, fs, fr, ys, yr, zus, zur, zds, zdr, s1s, s1r, s2s, s2r, s3s, s3r):
    r = lax.axis_index("row")
    c = lax.axis_index("col")
    core, x, zh = r % 2, (r // 2) % 4, r // 8
    a, b = c // 4, c % 4

    load_own = pltpu.make_async_copy(basis_ref, ox.at[pl.ds(HALO, ROWS)], lsem.at[0])
    load_own.start()
    load_s = pltpu.make_async_copy(stiff_ref, sv, lsem.at[1])
    load_s.start()

    def yb(d):
        return (b + d) % 4

    def ycol(d):
        return a * 4 + yb(d)

    def zcol(z):
        return z * 4 + b

    up_row, down_row = (r + 1) % 16, (r + 15) % 16
    barrier = pltpu.get_barrier_semaphore()

    def greet(i, carry):
        row = (r + i) % 16

        @pl.when(i > 0)
        def _():
            pl.semaphore_signal(barrier, inc=1, device_id=(row, c), device_id_type=MESH)

        for d in (1, 2, 3):
            pl.semaphore_signal(barrier, inc=1, device_id=(row, ycol(d)), device_id_type=MESH)
            pl.semaphore_signal(barrier, inc=1, device_id=(row, zcol((a + d) % 4)), device_id_type=MESH)
        return carry

    lax.fori_loop(0, 16, greet, 0)
    pl.semaphore_wait(barrier, 16 * 7 - 1)

    def remote(src, dst, ss, rs, dev):
        return pltpu.make_async_remote_copy(src_ref=src, dst_ref=dst, send_sem=ss, recv_sem=rs,
                                            device_id=dev, device_id_type=MESH)

    halo_up = remote(basis_ref.at[pl.ds(ROWS - HALO, HALO)], ox.at[pl.ds(0, HALO)], hs.at[0], hr.at[0], (up_row, c))
    halo_down = remote(basis_ref.at[pl.ds(0, HALO)], ox.at[pl.ds(ROWS + HALO, HALO)], hs.at[1], hr.at[1], (down_row, c))
    own_lo = basis_ref.at[pl.ds(0, HALF)]
    own_hi = basis_ref.at[pl.ds(HALF, HALF)]
    nxt, prv = (r, ycol(1)), (r, ycol(3))
    y_lo_n = remote(own_lo, ya.at[1, pl.ds(HALO, HALF)], ys.at[0], yr.at[0], nxt)
    y_hi_n = remote(own_hi, yh.at[1], ys.at[1], yr.at[1], nxt)
    y_hi_p = remote(own_hi, yh.at[0], ys.at[2], yr.at[2], prv)
    y_lo_p = remote(own_lo, ya.at[0, pl.ds(HALO, HALF)], ys.at[3], yr.at[3], prv)
    PIECE = HALF // 2
    y_lo_f = [remote(ya.at[1, pl.ds(HALO + p * PIECE, PIECE)], ya.at[2, pl.ds(HALO + p * PIECE, PIECE)],
                     ys.at[4 + p], yr.at[4 + p], nxt) for p in range(2)]
    y_hi_f = [remote(yh.at[0, pl.ds(p * PIECE, PIECE)], yh.at[2, pl.ds(p * PIECE, PIECE)],
                     ys.at[6 + p], yr.at[6 + p], prv) for p in range(2)]

    zup = (r, zcol((a + 1) % 4))
    zdn = (r, zcol((a + 3) % 4))
    DN = HALF + HALO
    UP_CUT = ((0, HALF // 2), (HALF // 2, HALF // 2))
    DN_CUT = ((0, HALF // 2 + BLOCK), (HALF // 2 + BLOCK, HALF // 2 + BLOCK))
    zu_cp, zd_cp = [], []
    for d in range(3):
        for p in range(2):
            o, n = UP_CUT[p]
            src = basis_ref.at[pl.ds(o, n)] if d == 0 else zu.at[d - 1, pl.ds(o, n)]
            zu_cp.append(remote(src, zu.at[d, pl.ds(o, n)], zus.at[2 * d + p], zur.at[2 * d + p], zup))
            o, n = DN_CUT[p]
            src = basis_ref.at[pl.ds(HALF - HALO + o, n)] if d == 0 else zd.at[d - 1, pl.ds(o, n)]
            zd_cp.append(remote(src, zd.at[d, pl.ds(o, n)], zds.at[2 * d + p], zdr.at[2 * d + p], zdn))

    y_lo_n.start()
    y_hi_p.start()
    for p in range(2):
        @pl.when(a < 3)
        def _():
            zu_cp[p].start()

        @pl.when(a > 0)
        def _():
            zd_cp[p].start()

    halo_up.start()
    halo_down.start()
    y_hi_n.start()
    y_lo_p.start()

    g[DEAD] = jnp.zeros((BLOCK, 2 * PAN), BF)

    halo_up.wait_recv()
    halo_down.wait_recv()
    fan_lo = [remote(ox.at[pl.ds(0, HALO)], ya.at[s - 1, pl.ds(0, HALO)], fs.at[s - 1], fr.at[s - 1], (r, ycol(dy)))
              for s, dy in ((1, 3), (2, 1), (3, 2))]
    fan_hi = [remote(ox.at[pl.ds(HALO + ROWS, HALO)], zd.at[d - 1, pl.ds(DN, HALO)], fs.at[2 + d], fr.at[2 + d],
                     (r, zcol((a + 4 - d) % 4))) for d in (1, 2, 3)]
    for cp in fan_lo:
        cp.start()
    for d in (1, 2, 3):
        @pl.when(a >= d)
        def _():
            fan_hi[d - 1].start()

    def apply(h, outs, lo=0, hi=NB):
        n = len(outs) * PAN

        def step(i, carry):
            row = h * NB + i
            lhs = jnp.concatenate([sv[0, row], sv[1, row]], axis=0)
            first = r * (2 * NB) + h * NB - 2
            picks = [i + 2] + [jnp.clip(cols_ref[s, row] - first, 0, DEAD) for s in range(1, CAP)]
            for s in range(3, CAP):
                picks[s] = jnp.where(s < counts_ref[row], picks[s], DEAD)
            picked = jnp.concatenate([g[k][:, 0:n] for k in picks], axis=0)
            res = jnp.dot(lhs, picked, preferred_element_type=F32).astype(BF)
            at = pl.ds(pl.multiple_of(i * BLOCK, BLOCK), BLOCK)
            for p, (ref, k) in enumerate(outs):
                for q in range(2):
                    ref[k, at, q * PAN:(q + 1) * PAN] = res[q * BLOCK:(q + 1) * BLOCK, p * PAN:(p + 1) * PAN]
            return carry

        lax.fori_loop(lo, hi, step, 0, unroll=UNROLL)

    def put(rows, at, lane):
        n = rows.shape[0] // BLOCK
        g[at:at + n, :, lane:lane + PAN] = rows.reshape(n, BLOCK, PAN)

    def take_y(s, lane):
        put(ya[s - 1], 0, lane)
        put(yh[s - 1, 0:HALO], DEAD - 2, lane)

    def turn_y(s, lo=0, hi=HALF):
        pt[0, s * PAN:(s + 1) * PAN, lo:hi] = ya[s - 1, HALO + lo:HALO + hi, :].T
        pt[1, s * PAN:(s + 1) * PAN, lo:hi] = yh[s - 1, lo:hi].T

    def keep(z, lo, res, more=False):
        for s in range(res.shape[0] // PAN):
            for half in range(2):
                at = s * PAN + half * HC
                rows = slice((lo + s) * HC, (lo + s + 1) * HC)
                if more:
                    acc[z, half, rows, :] += res[at:at + HC, :]
                else:
                    acc[z, half, rows, :] = res[at:at + HC, :]

    def down(d, lo, hi, k0=0, k1=HALF):
        res = jnp.dot(pt[1, lo * PAN:hi * PAN, k0:k1], az[d, k0:k1, :], preferred_element_type=F32)
        if d == 0:
            res += jnp.dot(pt[0, lo * PAN:hi * PAN, k0:k1], ap[0, k0:k1, :], preferred_element_type=F32)
        keep(a + d, lo, res, k0 > 0)

    def up(d, s, k0=0, k1=HALF):
        keep(a - d, s, jnp.dot(zt[d - 1, :, k0:k1], ap[s, k0:k1, :], preferred_element_type=F32), k0 > 0)

    def pass_on(d):
        for p in range(2 * d, 2 * d + 2):
            @pl.when(a > d)
            def _():
                zu_cp[p].wait_recv()

            @pl.when((a > d) & (a < 3))
            def _():
                zu_cp[p + 2].start()

            @pl.when(a + d < 3)
            def _():
                zd_cp[p].wait_recv()

            @pl.when((a + d < 3) & (a > 0))
            def _():
                zd_cp[p + 2].start()

    load_own.wait()
    load_s.wait()
    put(ox[0:EXT, :], 0, 0)
    apply(0, [(ap, 0)])
    pt[0, 0:PAN, :] = ox[HALO:HALO + HALF, :].T
    pt[1, 0:PAN, :] = ox[HALO + HALF:HALO + ROWS, :].T

    pass_on(0)

    put(ox[HALF:HALF + EXT, :], 0, 0)

    @pl.when(a < 3)
    def _():
        fan_hi[0].wait_recv()
        put(zd[0], 0, PAN)
        apply(1, [(az, 0), (az, 1)])

    @pl.when(a == 3)
    def _():
        apply(1, [(az, 0)])

    down(0, 0, 1)

    @pl.when(a < 3)
    def _():
        down(1, 0, 1)

    @pl.when(a > 0)
    def _():
        zt[0] = zu[0].T
        up(1, 0)

    y_lo_n.wait_recv()
    y_hi_p.wait_recv()
    for p in range(2):
        y_lo_f[p].start()
        y_hi_f[p].start()

    pass_on(1)
    y_hi_n.wait_recv()
    y_lo_p.wait_recv()
    for s in (1, 2):
        fan_lo[s - 1].wait_recv()
        turn_y(s)

    @pl.when(a > 0)
    def _():
        take_y(1, 0)
        take_y(2, PAN)
        apply(0, [(ap, 1), (ap, 2)])
        for s in (1, 2):
            up(1, s)

    @pl.when(a > 1)
    def _():
        zt[1] = zu[1].T
        for s in (0, 1, 2):
            up(2, s)

    down(0, 1, 3)

    @pl.when(a < 3)
    def _():
        down(1, 1, 3)

    @pl.when(a < 2)
    def _():
        fan_hi[1].wait_recv()
        put(zd[1], 0, 0)
        apply(1, [(az, 2)])
        down(2, 0, 3)

    EARLY, LATE = (0, 3), (3, 4)

    def each(fn, which):
        def step(z, carry):
            far = (z - a == 3) | (a - z == 3)
            if which == "early":
                @pl.when(jnp.logical_not(far))
                def _():
                    fn(z, 0, *EARLY)
            elif which == "late":
                @pl.when(far)
                def _():
                    fn(z, 0, *EARLY)
                fn(z, 1, *LATE)
            else:
                fn(z, 0, *EARLY)
                fn(z, 1, *LATE)
            return carry
        lax.fori_loop(0, 4, step, 0)

    def pair_copy(z, w, lo, hi):
        rows = pl.ds(lo * HC, (hi - lo) * HC)
        return remote(acc.at[z, 1 - core, rows], r1.at[z, rows], s1s.at[z, w], s1r.at[z, w],
                      (zh * 8 + x * 2 + (1 - core), c))

    def x_copy(z, w, lo, hi, d):
        rows = pl.ds(lo * QC, (hi - lo) * QC)
        return remote(s2.at[z, d - 1, rows], r2.at[z, d - 1, rows], s2s.at[z, w, d - 1], s2r.at[z, w, d - 1],
                      (zh * 8 + ((x + d) % 4) * 2 + core, c))

    def owner(z, s):
        y = (b + s + (s // 2) * (1 - 2 * (s % 2))) % 4
        left = jnp.where(z < a, z * 4 + b, a * 4 + y)
        right = jnp.where(z < a, a * 4 + y, z * 4 + b)
        place = jnp.where(z < a, 0, 2) + zh
        return left, right, place, (z != a) | (y <= b)

    share = pl.ds(pl.multiple_of(core * HC + x * QC, QC), QC)

    def last_copy(z, s, left, right, place):
        return remote(tot.at[z, s], fin.at[place, share], s3s.at[z, s], s3r.at[place], (left, right))

    def pair_send(z, w, lo, hi):
        pair_copy(z, w, lo, hi).start()

    def pair_sum(z, w, lo, hi):
        pair_copy(z, w, lo, hi).wait_recv()
        for s in range(lo, hi):
            for d in (1, 2, 3):
                rows = pl.ds(pl.multiple_of(s * HC + ((x + d) % 4) * QC, QC), QC)
                s2[z, d - 1, s * QC:(s + 1) * QC, :] = (acc[z, core, rows, :] + r1[z, rows, :]).astype(BF)
        for d in (1, 2, 3):
            x_copy(z, w, lo, hi, d).start()

    def x_sum(z, w, lo, hi):
        for d in (1, 2, 3):
            x_copy(z, w, lo, hi, d).wait_recv()
        for s in range(lo, hi):
            rows = pl.ds(pl.multiple_of(s * HC + x * QC, QC), QC)
            part = acc[z, core, rows, :] + r1[z, rows, :]
            for d in (1, 2, 3):
                part += r2[z, d - 1, s * QC:(s + 1) * QC, :].astype(F32)
            left, right, place, used = owner(z, s)
            here = (left == r) & (right == c)

            @pl.when(used & here)
            def _():
                fin[place, share, :] = part.astype(BF)

            @pl.when(used & jnp.logical_not(here))
            def _():
                tot[z, s] = part.astype(BF)
                last_copy(z, s, left, right, place).start()

    each(pair_send, "early")

    E0 = HALO + PIECE
    N0 = E0 // BLOCK - 4
    READY = DN_CUT[0][1] // BLOCK - 5
    for p in range(2):
        lo, hi = p * PIECE, (p + 1) * PIECE
        y_lo_f[p].wait_recv()
        y_hi_f[p].wait_recv()
        if p == 0:
            fan_lo[2].wait_recv()
        turn_y(3, lo, hi)

        @pl.when(a > 0)
        def _():
            if p == 0:
                put(ya[2, 0:E0], 0, 0)
                apply(0, [(ap, 3)], 0, N0)
            else:
                put(ya[2, E0:HALO + HALF], E0 // BLOCK, 0)
                put(yh[2, 0:HALO], DEAD - 2, 0)
                apply(0, [(ap, 3)], N0, NB)

        @pl.when(a == 3)
        def _():
            zu_cp[4 + p].wait_recv()
            zt[2, :, lo:hi] = zu[2, lo:hi].T
            for s in (0, 1, 2):
                up(3, s, lo, hi)

        @pl.when(a == 0)
        def _():
            zd_cp[4 + p].wait_recv()
            o, n = DN_CUT[p]
            put(zd[2, o:o + n], o // BLOCK, 0)
            if p == 0:
                apply(1, [(az, 3)], 0, READY)
                down(3, 0, 3, 0, READY * BLOCK)
            else:
                fan_hi[2].wait_recv()
                put(zd[2, DN:EXT], DEAD - 2, 0)
                apply(1, [(az, 3)], READY, NB)
                down(3, 0, 3, READY * BLOCK, HALF)
                down(3, 3, 4)

        for d in (1, 2, 3):
            @pl.when(a >= d)
            def _():
                if p == 0:
                    up(d, 3, 0, N0 * BLOCK)
                else:
                    up(d, 3, N0 * BLOCK, HALF)

        down(0, 3, 4, lo, hi)
        for d in (1, 2):
            @pl.when(a + d < 4)
            def _():
                down(d, 3, 4, lo, hi)

        if p == 0:
            each(pair_sum, "early")

    each(pair_send, "late")
    each(pair_sum, "late")
    each(x_sum, "early")
    each(x_sum, "late")

    zi, yi = r // 4, r % 4
    cross = zi < a
    plane = (zi == a) & (yi <= b)

    def fin_wait(place, rows):
        part = fin.at[place, pl.ds(0, rows)]
        remote(part, part, s3s.at[0, 0], s3r.at[place], (r, other)).wait_recv()

    other = ycol(1)
    for place in range(4):
        if place < 2:
            wanted, here = cross, (yi == b) & (zh == place)
        else:
            wanted, here = cross | plane, plane & (zh == place - 2)

        @pl.when(wanted & here)
        def _():
            fin_wait(place, PAN - QC)

        @pl.when(wanted & jnp.logical_not(here))
        def _():
            fin_wait(place, PAN)

    @pl.when(cross)
    def _():
        out_ref[...] = (fin[0].astype(F32) + fin[1].astype(F32)) + (fin[2].astype(F32) + fin[3].astype(F32))

    @pl.when(plane)
    def _():
        out_ref[...] = fin[2].astype(F32) + fin[3].astype(F32)

    @pl.when(jnp.logical_not(cross | plane))
    def _():
        out_ref[...] = jnp.zeros_like(out_ref)

    for cp in [halo_up, halo_down, y_lo_n, y_hi_n, y_hi_p, y_lo_p] + y_lo_f + y_hi_f + fan_lo:
        cp.wait_send()
    for d in (1, 2, 3):
        @pl.when(a >= d)
        def _():
            fan_hi[d - 1].wait_send()

        @pl.when((a >= d - 1) & (a < 3))
        def _():
            zu_cp[2 * d - 2].wait_send()
            zu_cp[2 * d - 1].wait_send()

        @pl.when((a + d - 1 <= 3) & (a > 0))
        def _():
            zd_cp[2 * d - 2].wait_send()
            zd_cp[2 * d - 1].wait_send()

    def drain(z, w, lo, hi):
        pair_copy(z, w, lo, hi).wait_send()
        for d in (1, 2, 3):
            x_copy(z, w, lo, hi, d).wait_send()
        for s in range(lo, hi):
            left, right, place, used = owner(z, s)

            @pl.when(used & jnp.logical_not((left == r) & (right == c)))
            def _():
                last_copy(z, s, left, right, place).wait_send()

    each(drain, "all")


def shards(basis, stiffness, block_cols, block_counts):
    dma = pltpu.SemaphoreType.DMA
    out = pl.pallas_call(
        kernel,
        out_shape=jax.ShapeDtypeStruct((PAN, 2 * PAN), F32),
        in_specs=[
            pl.BlockSpec(memory_space=pltpu.SMEM),
            pl.BlockSpec(memory_space=pltpu.SMEM),
            pl.BlockSpec(memory_space=pltpu.HBM),
            pl.BlockSpec(memory_space=pltpu.HBM),
        ],
        out_specs=pl.BlockSpec(memory_space=pltpu.VMEM),
        scratch_shapes=[
            pltpu.VMEM((2, 2 * NB, BLOCK, CAP * BLOCK), BF),
            pltpu.VMEM((ROWS + 2 * HALO, PAN), BF),
            pltpu.VMEM((3, HALO + HALF, PAN), BF),
            pltpu.VMEM((3, HALF, PAN), BF),
            pltpu.VMEM((3, HALF, PAN), BF),
            pltpu.VMEM((3, EXT, PAN), BF),
            pltpu.VMEM((DEAD + 1, BLOCK, 2 * PAN), BF),
            pltpu.VMEM((2, 4 * PAN, HALF), BF),
            pltpu.VMEM((3, PAN, HALF), BF),
            pltpu.VMEM((4, HALF, 2 * PAN), BF),
            pltpu.VMEM((4, HALF, 2 * PAN), BF),
            pltpu.VMEM((4, 2, 4 * HC, 2 * PAN), F32),
            pltpu.VMEM((4, 4 * HC, 2 * PAN), F32),
            pltpu.VMEM((4, 3, 4 * QC, 2 * PAN), BF),
            pltpu.VMEM((4, 3, 4 * QC, 2 * PAN), BF),
            pltpu.VMEM((4, 4, QC, 2 * PAN), BF),
            pltpu.VMEM((4, PAN, 2 * PAN), BF),
            dma((2,)), dma((2,)), dma((2,)), dma((6,)), dma((6,)), dma((8,)), dma((8,)),
            dma((6,)), dma((6,)), dma((6,)), dma((6,)),
            dma((4, 2)), dma((4, 2)), dma((4, 2, 3)), dma((4, 2, 3)), dma((4, 4)), dma((4,)),
        ],
        compiler_params=pltpu.CompilerParams(
            collective_id=0, has_side_effects=True, vmem_limit_bytes=56 * 2**20),
        cost_estimate=pl.CostEstimate(flops=8 * 10**9, bytes_accessed=10 * 2**20, transcendentals=0),
    )(block_cols.T, block_counts, basis, stiffness)
    return out.reshape(PAN, 2, PAN)


def solution(mesh):
    return jax.shard_map(
        shards,
        mesh=mesh,
        in_specs=(P("row", "col"), P(None, "row", None, None), P("row", None), P("row")),
        out_specs=P("row", None, "col"),
        check_vma=False,
    )
```
